1024 devices in a mesh: group: 64 (over z, core), node: 16 (over y, x).
Axes of the slice: x: 4, y: 4, z: 32, core: 2. Of those that a mesh axis runs over, the one named last changes fastest.
Arguments:
- grads: bfloat16 [393216, 1280], P(('group', 'node')), may hold values from -6 to 6
- merge_slot: int32 [393216], P(('group', 'node')), may hold values from 0 to 383, as said below
- slot_row: int32 [393216], P(('group', 'node')), may hold values from 0 to 63, as said below
- params: float32 [65536, 1280], P(('group', 'node')), may hold values from -6 to 6
- moment: float32 [65536, 1280], P(('group', 'node')), may hold values from -4 to 4
- second: float32 [65536, 1280], P(('group', 'node')), may hold values from 0.01 to 1
Outputs:
- new_params: float32 [65536, 1280], P(('group', 'node'))
- new_moment: float32 [65536, 1280], P(('group', 'node'))
- new_second: float32 [65536, 1280], P(('group', 'node'))
The draws below stay inside these ranges and needn't reach their ends.
Inputs may be any that keep to these rules, and one draw needn't show every extreme that they name: `merge_slot`: tokens of one merging device that share a slot share a table row; slot s of merging device (g, k) goes to owner (s // 6, k); slot 0 and slot 383 are used on every merging device. `slot_row`: within each aligned block of 6 slots of one merging device the rows are distinct.
All inputs are finite; a program needn't handle non-finite values.
Results may differ from the reference program's by a relative error of at most 0.0003.
Values may be sent and summed in bfloat16 or wider, within the bound.
A program may use at most 128 MiB of HBM per device.

```python
import math
import jax
import jax.numpy as jnp
from jax import lax

D = 1280
TOK_DEV = 384
ROWS_DEV = 64
TOKENS = 393216
ROWS = 65536
N_GROUP = 64
N_NODE = 16


def draw_merge_slot(key, part):
    key = jax.random.fold_in(key, 11)
    blk = TOK_DEV // N_NODE
    cap = TOK_DEV // N_GROUP
    mergers = N_GROUP * N_NODE
    key_a, key_b, key_c, key_d = jax.random.split(key, 4)
    first = jax.random.randint(key_a, (mergers, TOK_DEV), 0, N_GROUP)
    second = jax.random.randint(key_b, (mergers, TOK_DEV), 0, N_GROUP)
    heavy = first * second // N_GROUP
    orders = jax.vmap(lambda kk: jax.random.permutation(kk, N_GROUP))(jax.random.split(key_c, mergers))
    target = jnp.take_along_axis(orders, heavy, axis=1)
    slot = target * cap + jax.random.randint(key_d, (mergers, TOK_DEV), 0, cap)
    slot = slot.at[:, 0].set(0)
    slot = slot.at[:, TOK_DEV - 1].set(TOK_DEV - 1)
    slot = slot.reshape(N_GROUP, N_NODE, N_NODE, blk).transpose(0, 2, 1, 3).reshape(-1)
    return slot.astype(jnp.int32)


def draw_slot_row(key, part):
    key = jax.random.fold_in(key, 23)
    cap = TOK_DEV // N_GROUP
    count = N_GROUP * N_NODE * N_GROUP
    keys = jax.random.split(key, count)
    picked = jax.vmap(lambda kk: jax.random.permutation(kk, ROWS_DEV)[:cap])(keys)
    return picked.reshape(-1).astype(jnp.int32)


def block_levels(key, dims, cuts, low, largest):
    def one(position, parts):
        heights = jax.random.uniform(jax.random.fold_in(jax.random.fold_in(key, 6), position), (parts,), jnp.float32, low / len(cuts), largest / len(cuts))
        return jnp.repeat(jnp.exp(heights), dims[position] // parts).reshape((-1,) + (1,) * (len(dims) - position - 1))

    level = one(*cuts[0])
    for cut in cuts[1:]:
        level = level * one(*cut)
    return level


def centred(rng, extent, deviation, most, cuts=(), kind=jnp.bfloat16):
    loudness = block_levels(rng, extent, cuts, -0.22, 0.18) if cuts else 1.0
    result = jax.random.normal(rng, extent, jnp.float32) * deviation * loudness
    return jnp.minimum(jnp.maximum(result, -most), most).astype(kind)


def setup_inputs(seed: int = 0) -> dict:
    key_of = jax.random.split(jax.random.key(seed), 7)
    return {
        "grads": centred(key_of[0], (TOKENS, D), 1.0, 6.0, ((0, 1024),)),
        "merge_slot": draw_merge_slot(jax.random.fold_in(key_of[6], 71), 0),
        "slot_row": draw_slot_row(jax.random.fold_in(key_of[6], 71), 0),
        "params": centred(key_of[3], (ROWS, D), 1.0, 6.0, ((0, 1024),), jnp.float32),
        "moment": centred(key_of[4], (ROWS, D), 0.5, 4.0, ((0, 1024),), jnp.float32),
        "second": jnp.clip(jnp.exp(math.log(1.0) - 4.6051702 * jax.random.uniform(key_of[5], (ROWS, D), jnp.float32) ** block_levels(key_of[5], (ROWS, D), ((0, 1024),), -0.2, 0.2)), 0.01, 1.0),
    }


def reference(grads, merge_slot, slot_row, params, moment, second):
    devices = N_GROUP * N_NODE
    blk = TOK_DEV // N_NODE
    cap = TOK_DEV // N_GROUP
    index = jnp.arange(TOKENS, dtype=jnp.int32)
    device = index // TOK_DEV
    group_of = device // N_NODE
    block = index % TOK_DEV // blk
    merger = group_of * N_NODE + block
    local = slot_row[(merger * TOK_DEV + merge_slot).astype(jnp.int32)]
    row = ((merge_slot // cap * N_NODE + block) * ROWS_DEV + local).astype(jnp.int32)
    grad_blocks = grads.reshape(devices, TOK_DEV, D)
    row_blocks = row.reshape(devices, TOK_DEV)

    def accumulate(total, pieces):
        piece, rows_here = pieces
        return (total.at[rows_here].add(piece.astype(jnp.float32)), None)
    grad, unused = lax.scan(accumulate, jnp.zeros((ROWS, D), jnp.float32), (grad_blocks, row_blocks))
    new_moment = 0.9 * moment + 0.1 * grad
    new_second = 0.999 * second + 0.001 * grad * grad
    first_fix = 1.0 - 0.9 ** 10
    second_fix = 1.0 - 0.999 ** 10
    new_params = params - 0.1 * (new_moment / first_fix) / (jnp.sqrt(new_second / second_fix) + 1e-08)
    return (new_params, new_moment, new_second)
```

```python
import functools

import jax
import jax.numpy as jnp
from jax import lax
from jax.experimental import pallas as pl
from jax.experimental.pallas import tpu as pltpu
from jax.sharding import PartitionSpec as P

MESH = pl.DeviceIdType.MESH
LANES = 128
PAIR = 2 * LANES
SUBS = (3, 2)
FINE = 64.0
TOP = 32600.0
LONGER, SHORTER = 0, 1


def block_rows(chunks, rows):
    return -(-(chunks * rows + chunks) // 8) * 8


def quotient(x, by, limit):
    magic = -(-65536 // by)
    assert all((v * magic) >> 16 == v // by for v in range(limit))
    return (x * magic) >> 16


def low_half(p):
    return (p << 16) >> 16


def pack(hi, lo):
    return (hi << 16) | (lo & 0xFFFF)


def nearest(x):
    return jnp.floor(x + 0.5).astype(jnp.int32)


def level_of(x):
    most = jnp.max(jnp.abs(x), axis=0, keepdims=True)
    return jnp.ceil(jnp.log2(jnp.maximum(most, 1e-30)) * FINE)


def quantise(x):
    level = level_of(x)
    q = nearest(x * (jnp.exp2(level * (-1.0 / FINE)) * TOP))
    return q, level.astype(jnp.int32)


def step_size(level):
    return jnp.exp2(level.astype(jnp.float32) * (1.0 / FINE)) * (1.0 / TOP)


def kernel(
    cfg,
    grads,
    slots,
    slot_row,
    out,
    tok3,
    slot_in,
    tok,
    code,
    contrib,
    slot_mat,
    *rest,
):
    n_group, n_node, rows, toks, width = cfg
    n_sub = len(SUBS)
    sends, rest = rest[:n_sub], rest[n_sub:]
    recvs, rest = rest[:n_sub], rest[n_sub:]
    (
        slot_send_sem,
        slot_recv_sem,
        tok_send_sem,
        tok_recv_sem,
        local_sem,
        pair_send_sem,
        pair_recv_sem,
        ring_send_sem,
        ring_recv_sem,
    ) = rest
    nz = n_group // 2
    hops = (nz // 2, nz // 2 - 1)
    blk = toks // n_node
    cap = toks // n_group
    starts = [PAIR * sum(SUBS[:i]) for i in range(n_sub)]
    cols = [slice(starts[i], starts[i] + PAIR * SUBS[i]) for i in range(n_sub)]

    group = lax.axis_index("group")
    node = lax.axis_index("node")
    z, c = lax.div(group, 2), lax.rem(group, 2)
    sign = 1 - 2 * c
    toward = (sign, -sign)

    def at_z(pos):
        return lax.rem(pos + 2 * nz, nz)

    partner = (z * 2 + 1 - c, node)
    ahead = [(at_z(z + toward[d]) * 2 + c, node) for d in (LONGER, SHORTER)]

    barrier = pltpu.get_barrier_semaphore()

    @pl.loop(1, n_node)
    def _(j):
        pl.semaphore_signal(
            barrier,
            inc=1,
            device_id=(group, lax.rem(node + j, n_node)),
            device_id_type=MESH,
        )

    for other in (partner, *ahead):
        pl.semaphore_signal(barrier, inc=1, device_id=other, device_id_type=MESH)
    pl.semaphore_wait(barrier, n_node + 2)

    def slot_copy(j):
        peer = lax.rem(node + j, n_node)
        return pltpu.make_async_remote_copy(
            src_ref=slots,
            dst_ref=slot_in.at[node],
            send_sem=slot_send_sem.at[j],
            recv_sem=slot_recv_sem.at[node],
            device_id=(group, peer),
            device_id_type=MESH,
        )

    def slot_arrival(j):
        peer = lax.rem(node + j, n_node)
        return pltpu.make_async_remote_copy(
            src_ref=slots,
            dst_ref=slot_in.at[peer],
            send_sem=slot_send_sem.at[j],
            recv_sem=slot_recv_sem.at[peer],
            device_id=(group, peer),
            device_id_type=MESH,
        )

    def tok_copy(i, j):
        peer = lax.rem(node + j, n_node)
        return pltpu.make_async_remote_copy(
            src_ref=grads.at[peer, :, cols[i]],
            dst_ref=tok3.at[node, :, cols[i]],
            send_sem=tok_send_sem.at[i, j],
            recv_sem=tok_recv_sem.at[i, node],
            device_id=(group, peer),
            device_id_type=MESH,
        )

    def tok_arrival(i, j):
        peer = lax.rem(node + j, n_node)
        return pltpu.make_async_remote_copy(
            src_ref=grads.at[peer, :, cols[i]],
            dst_ref=tok3.at[peer, :, cols[i]],
            send_sem=tok_send_sem.at[i, j],
            recv_sem=tok_recv_sem.at[i, peer],
            device_id=(group, peer),
            device_id_type=MESH,
        )

    own_tok = pltpu.make_async_copy(grads.at[node], tok3.at[node], local_sem.at[0])
    own_slot = pltpu.make_async_copy(slots, slot_in.at[node], local_sem.at[1])

    @pl.loop(1, n_node)
    def _(j):
        slot_copy(j).start()

    own_slot.start()
    own_tok.start()
    for i in range(n_sub):

        @pl.loop(1, n_node)
        def _(j, i=i):
            tok_copy(i, j).start()

    own_slot.wait()

    @pl.loop(1, n_node)
    def _(j):
        slot_arrival(j).wait_recv()

    for n in range(n_node):
        slot_mat[n : n + 1, :] = slot_in[n]
    slot = slot_mat[...]
    owner = quotient(slot, cap, toks)
    place = slot - owner * cap
    lane = lax.broadcasted_iota(jnp.int32, (toks, toks), 1)
    sub = lax.broadcasted_iota(jnp.int32, (toks, toks), 0)
    mine = (sub - node * blk == lane - quotient(lane, blk, toks) * blk).astype(
        jnp.bfloat16
    )
    lane = lax.broadcasted_iota(jnp.int32, (n_node, toks), 1)
    source = lax.broadcasted_iota(jnp.int32, (n_node, toks), 0)
    here = (quotient(lane, blk, toks) == source).astype(jnp.float32)

    def pick(values):
        moved = jnp.dot(
            values.astype(jnp.float32).astype(jnp.bfloat16),
            mine,
            preferred_element_type=jnp.float32,
        )
        return jnp.sum(moved * here, axis=0, keepdims=True)

    owner = pick(owner)
    index = owner * float(cap) + pick(place)
    onehot = (index == sub.astype(jnp.float32)).astype(jnp.bfloat16)
    table = jnp.broadcast_to(slot_row[...], (8, toks)).astype(jnp.float32)
    row = jnp.dot(
        table.astype(jnp.bfloat16), onehot, preferred_element_type=jnp.float32
    )
    code[0] = owner * float(rows) + row[0:1, :]

    pair_code = pltpu.make_async_remote_copy(
        src_ref=code.at[0],
        dst_ref=code.at[1],
        send_sem=pair_send_sem.at[n_sub],
        recv_sem=pair_recv_sem.at[n_sub],
        device_id=partner,
        device_id_type=MESH,
    )
    pair_code.start()

    def pair_copy(i):
        return pltpu.make_async_remote_copy(
            src_ref=tok.at[0:toks, cols[i]],
            dst_ref=tok.at[toks : 2 * toks, cols[i]],
            send_sem=pair_send_sem.at[i],
            recv_sem=pair_recv_sem.at[i],
            device_id=partner,
            device_id_type=MESH,
        )

    def onehot_of(owner_z):
        base = ((owner_z * 2 + c) * rows).astype(jnp.float32)
        ids = lax.broadcasted_iota(jnp.int32, (rows, toks), 0).astype(jnp.float32)
        ids = ids + base
        return jnp.concatenate(
            [(code[h] == ids).astype(jnp.bfloat16) for h in (0, 1)], axis=1
        )

    def add_up(dst, owner_z, i):
        onehot = onehot_of(owner_z)
        for k in range(SUBS[i]):
            at = starts[i] + k * PAIR
            dst[:, at : at + PAIR] = jnp.dot(
                onehot, tok[:, at : at + PAIR], preferred_element_type=jnp.float32
            )

    def arrived(ref, i, k):
        levels = ref[rows * SUBS[i] + k : rows * SUBS[i] + k + 1, :]
        packed = ref[rows * k : rows * (k + 1), :]
        hi = (packed >> 16).astype(jnp.float32) * step_size(levels >> 16)
        lo = low_half(packed).astype(jnp.float32) * step_size(low_half(levels))
        return hi, lo

    def ring_copy(i, d, s):
        return pltpu.make_async_remote_copy(
            src_ref=sends[i].at[d, lax.rem(s, 2)],
            dst_ref=recvs[i].at[d, s],
            send_sem=ring_send_sem.at[i, d, lax.rem(s, 2)],
            recv_sem=ring_recv_sem.at[i, d, s],
            device_id=ahead[d],
            device_id_type=MESH,
        )

    def ring_step(i, d, s, first):
        owner_z = at_z(z + toward[d] * (hops[d] - s))
        add_up(contrib, owner_z, i)
        if not first:
            ring_copy(i, d, s - 1).wait_recv()

            @pl.when(s >= 2)
            def _():
                ring_copy(i, d, s - 2).wait_send()

        send = sends[i].at[d, lax.rem(s, 2)]
        for k in range(SUBS[i]):
            at = starts[i] + k * PAIR
            hi = contrib[:, at : at + LANES]
            lo = contrib[:, at + LANES : at + PAIR]
            if not first:
                more_hi, more_lo = arrived(recvs[i].at[d, s - 1], i, k)
                hi, lo = hi + more_hi, lo + more_lo
            q_hi, level_hi = quantise(hi)
            q_lo, level_lo = quantise(lo)
            send[rows * k : rows * (k + 1), :] = pack(q_hi, q_lo)
            send[rows * SUBS[i] + k : rows * SUBS[i] + k + 1, :] = pack(
                level_hi, level_lo
            )
        ring_copy(i, d, s).start()

    for i in range(n_sub):
        if i == 0:
            own_tok.wait()

        @pl.loop(1, n_node)
        def _(j, i=i):
            tok_arrival(i, j).wait_recv()

        tok[0:toks, cols[i]] = jnp.concatenate(
            [tok3[n, :, cols[i]].astype(jnp.float32) for n in range(n_node)], axis=0
        ).astype(jnp.bfloat16)
        pair_copy(i).start()
        if i == 0:
            pair_code.wait_recv()
        pair_copy(i).wait_recv()
        for d in (LONGER, SHORTER):
            ring_step(i, d, 0, True)

    @pl.loop(1, hops[SHORTER])
    def _(s):
        for i in range(n_sub):
            for d in (LONGER, SHORTER):
                ring_step(i, d, s, False)

    for i in range(n_sub):
        ring_step(i, LONGER, hops[LONGER] - 1, False)
    for i in range(n_sub):
        add_up(contrib, z, i)
    for i in range(n_sub):
        for d in (LONGER, SHORTER):
            ring_copy(i, d, hops[d] - 1).wait_recv()
        for k in range(SUBS[i]):
            at = starts[i] + k * PAIR
            hi = contrib[:, at : at + LANES]
            lo = contrib[:, at + LANES : at + PAIR]
            for d in (LONGER, SHORTER):
                more_hi, more_lo = arrived(recvs[i].at[d, hops[d] - 1], i, k)
                hi, lo = hi + more_hi, lo + more_lo
            out[:, at : at + LANES] = hi
            out[:, at + LANES : at + PAIR] = lo

    @pl.loop(1, n_node)
    def _(j):
        slot_copy(j).wait_send()
        for i in range(n_sub):
            tok_copy(i, j).wait_send()

    pair_code.wait_send()
    for i in range(n_sub):
        pair_copy(i).wait_send()
        for d in (LONGER, SHORTER):
            for s in range(max(hops[d] - 2, 0), hops[d]):
                ring_copy(i, d, s).wait_send()


def summed(grads, merge_slot, slot_row, n_group, n_node, rows):
    toks, width = grads.shape
    blk = toks // n_node
    assert width == PAIR * sum(SUBS)
    nz = n_group // 2
    hops = nz // 2
    n_sub = len(SUBS)
    cfg = (n_group, n_node, rows, toks, width)
    i32, f32, bf16 = jnp.int32, jnp.float32, jnp.bfloat16
    vmem, dma = pltpu.VMEM, pltpu.SemaphoreType.DMA
    return pl.pallas_call(
        functools.partial(kernel, cfg),
        out_shape=jax.ShapeDtypeStruct((rows, width), f32),
        in_specs=[
            pl.BlockSpec(memory_space=pl.ANY),
            pl.BlockSpec(memory_space=vmem),
            pl.BlockSpec(memory_space=vmem),
        ],
        out_specs=pl.BlockSpec(memory_space=vmem),
        scratch_shapes=[
            vmem((n_node, blk, width), bf16),
            vmem((n_node, 1, toks), i32),
            vmem((2 * toks, width), bf16),
            vmem((2, 1, toks), f32),
            vmem((rows, width), f32),
            vmem((n_node, toks), i32),
            *[vmem((2, 2, block_rows(m, rows), LANES), i32) for m in SUBS],
            *[vmem((2, hops, block_rows(m, rows), LANES), i32) for m in SUBS],
            dma((n_node,)),
            dma((n_node,)),
            dma((n_sub, n_node)),
            dma((n_sub, n_node)),
            dma((2,)),
            dma((n_sub + 1,)),
            dma((n_sub + 1,)),
            dma((n_sub, 2, 2)),
            dma((n_sub, 2, hops)),
        ],
        compiler_params=pltpu.CompilerParams(
            collective_id=0, has_side_effects=True, vmem_limit_bytes=40 * 1024 * 1024
        ),
        name="ring_sums",
    )(
        grads.reshape(n_node, blk, width),
        merge_slot.reshape(1, toks),
        slot_row.reshape(1, toks),
    )


def on_device(n_group, n_node, grads, merge_slot, slot_row, params, moment, second):
    grad = summed(grads, merge_slot, slot_row, n_group, n_node, params.shape[0])
    new_moment = 0.9 * moment + 0.1 * grad
    new_second = 0.999 * second + 0.001 * grad * grad
    first_fix = 1.0 - 0.9**10
    second_fix = 1.0 - 0.999**10
    new_params = params - 0.1 * (new_moment / first_fix) / (
        jnp.sqrt(new_second / second_fix) + 1e-08
    )
    return (new_params, new_moment, new_second)


def solution(mesh):
    whole, flat = P(("group", "node"), None), P(("group", "node"))
    return jax.shard_map(
        functools.partial(on_device, mesh.shape["group"], mesh.shape["node"]),
        mesh=mesh,
        in_specs=(whole, flat, flat, whole, whole, whole),
        out_specs=(whole, whole, whole),
        check_vma=False,
    )
```

```python
import functools

import jax
import jax.numpy as jnp
from jax import lax
from jax.experimental import pallas as pl
from jax.experimental.pallas import tpu as pltpu
from jax.sharding import PartitionSpec as P

MESH = pl.DeviceIdType.MESH
LANES = 128
PIECE = 2 * LANES
FINE = 64.0
TOP = 32600.0
LONGER, SHORTER = 0, 1


def quotient(x, by, limit):
    magic = -(-65536 // by)
    assert all((v * magic) >> 16 == v // by for v in range(limit))
    return (x * magic) >> 16


def low_half(p):
    return (p << 16) >> 16


def pack(hi, lo):
    return (hi << 16) | (lo & 0xFFFF)


def nearest(x):
    return jnp.floor(x + 0.5).astype(jnp.int32)


def halves(x):
    return x[..., :LANES], x[..., LANES:]


def quantise(x):
    most = jnp.max(jnp.abs(x), axis=-2, keepdims=True)
    level = jnp.ceil(jnp.log2(jnp.maximum(most, 1e-30)) * FINE)
    q = nearest(x * (jnp.exp2(level * (-1.0 / FINE)) * TOP))
    return pack(*halves(q)), pack(*halves(level.astype(jnp.int32)))


def step_size(level):
    return jnp.exp2(level.astype(jnp.float32) * (1.0 / FINE)) * (1.0 / TOP)


def unpack(packed, levels):
    hi = (packed >> 16).astype(jnp.float32) * step_size(levels >> 16)
    lo = low_half(packed).astype(jnp.float32) * step_size(low_half(levels))
    return jnp.concatenate([hi, lo], axis=-1)


def plan(n_group, toks):
    nz = n_group // 2
    hops = (nz // 2, nz // 2 - 1)
    relay = 12 if nz == 32 else max(nz // 2 - 2, 1)
    far = (hops[0] - relay, hops[1] - relay)
    both = 2 * (toks // n_group)
    return nz, relay, far, both, -(-(both + 2) // 8) * 8


def kernel(
    cfg,
    grads,
    slots,
    slot_row,
    out,
    tok3,
    slot_in,
    tok,
    code,
    slot_mat,
    onehots,
    contrib,
    far_onehot,
    far_ids,
    far_out,
    far_in,
    ring_out,
    ring_in,
    slot_send_sem,
    slot_recv_sem,
    tok_send_sem,
    tok_recv_sem,
    local_sem,
    pair_send_sem,
    pair_recv_sem,
    far_send_sem,
    far_recv_sem,
    ring_send_sem,
    ring_recv_sem,
):
    n_group, n_node, rows, toks, width = cfg
    nz, relay, far, both, far_rows = plan(n_group, toks)
    f32, bf16 = jnp.float32, jnp.bfloat16
    pieces = width // PIECE
    blk = toks // n_node
    cap = toks // n_group
    cols = [slice(PIECE * i, PIECE * (i + 1)) for i in range(pieces)]
    ways = (LONGER, SHORTER)
    far_all = far[LONGER] + far[SHORTER]

    group = lax.axis_index("group")
    node = lax.axis_index("node")
    z, c = lax.div(group, 2), lax.rem(group, 2)
    sign = 1 - 2 * c
    toward = (sign, -sign)

    def at_z(pos):
        return lax.rem(pos + 2 * nz, nz)

    def along(d, distance):
        return at_z(z + toward[d] * distance) * 2 + c

    partner = (z * 2 + 1 - c, node)

    far_in[...] = jnp.zeros_like(far_in)
    barrier = pltpu.get_barrier_semaphore()

    @pl.loop(1, n_node)
    def _(j):
        pl.semaphore_signal(
            barrier,
            inc=1,
            device_id=(group, lax.rem(node + j, n_node)),
            device_id_type=MESH,
        )

    near = max(far[LONGER], 1)
    pl.semaphore_signal(barrier, inc=1, device_id=partner, device_id_type=MESH)
    for d in ways:

        @pl.loop(1, near + 1)
        def _(j, d=d):
            pl.semaphore_signal(
                barrier, inc=1, device_id=(along(d, j), node), device_id_type=MESH
            )

    pl.semaphore_wait(barrier, n_node + 2 * near)

    def slot_copy(j, landing):
        peer = lax.rem(node + j, n_node)
        at = peer if landing else node
        return pltpu.make_async_remote_copy(
            src_ref=slots,
            dst_ref=slot_in.at[at],
            send_sem=slot_send_sem.at[j],
            recv_sem=slot_recv_sem.at[at],
            device_id=(group, peer),
            device_id_type=MESH,
        )

    def tok_copy(i, j, landing):
        peer = lax.rem(node + j, n_node)
        at = peer if landing else node
        return pltpu.make_async_remote_copy(
            src_ref=grads.at[peer, :, cols[i]],
            dst_ref=tok3.at[at, :, cols[i]],
            send_sem=tok_send_sem.at[i, j],
            recv_sem=tok_recv_sem.at[i, at],
            device_id=(group, peer),
            device_id_type=MESH,
        )

    own_tok = pltpu.make_async_copy(grads.at[node], tok3.at[node], local_sem.at[0])
    own_slot = pltpu.make_async_copy(slots, slot_in.at[node], local_sem.at[1])

    @pl.loop(1, n_node)
    def _(j):
        slot_copy(j, False).start()

    own_slot.start()
    own_tok.start()
    for i in range(pieces):

        @pl.loop(1, n_node)
        def _(j, i=i):
            tok_copy(i, j, False).start()

    own_slot.wait()

    @pl.loop(1, n_node)
    def _(j):
        slot_copy(j, True).wait_recv()

    for n in range(n_node):
        for k in range(toks // LANES):
            slot_mat[n : n + 1, k * LANES : (k + 1) * LANES] = slot_in[n, k : k + 1, :]
    slot = slot_mat[...]
    owner = quotient(slot, cap, toks)
    place = slot - owner * cap
    lane = lax.broadcasted_iota(jnp.int32, (toks, toks), 1)
    sub = lax.broadcasted_iota(jnp.int32, (toks, toks), 0)
    mine = sub - node * blk == lane - quotient(lane, blk, toks) * blk
    mine = mine.astype(f32).astype(bf16)
    lane = lax.broadcasted_iota(jnp.int32, (n_node, toks), 1)
    source = lax.broadcasted_iota(jnp.int32, (n_node, toks), 0)
    here = (quotient(lane, blk, toks) == source).astype(f32)

    def pick(values):
        moved = jnp.dot(
            values.astype(f32).astype(bf16), mine, preferred_element_type=f32
        )
        return jnp.sum(moved * here, axis=0, keepdims=True)

    owner = pick(owner)
    index = owner * float(cap) + pick(place)
    onehot = (index == sub.astype(f32)).astype(f32).astype(bf16)
    table = jnp.concatenate(
        [slot_row[k : k + 1, :] for k in range(toks // LANES)], axis=1
    ).astype(f32)
    row = jnp.dot(
        jnp.broadcast_to(table, (8, toks)).astype(bf16),
        onehot,
        preferred_element_type=f32,
    )
    code[0, 0:1, :] = owner * float(rows) + row[0:1, :]
    code[0, 1:2, :] = index
    code[0, 2:3, :] = table

    pair_code = pltpu.make_async_remote_copy(
        src_ref=code.at[0],
        dst_ref=code.at[1],
        send_sem=pair_send_sem.at[pieces],
        recv_sem=pair_recv_sem.at[pieces],
        device_id=partner,
        device_id_type=MESH,
    )
    pair_code.start()

    def pair_copy(i):
        return pltpu.make_async_remote_copy(
            src_ref=tok.at[0:toks, cols[i]],
            dst_ref=tok.at[toks : 2 * toks, cols[i]],
            send_sem=pair_send_sem.at[i],
            recv_sem=pair_recv_sem.at[i],
            device_id=partner,
            device_id_type=MESH,
        )

    def far_copy(i, k):
        d, j = (LONGER, k) if k < far[LONGER] else (SHORTER, k - far[LONGER])
        return pltpu.make_async_remote_copy(
            src_ref=far_out.at[i, k, 0 : both + 2],
            dst_ref=far_in.at[i, k, 0 : both + 2],
            send_sem=far_send_sem.at[i, k],
            recv_sem=far_recv_sem.at[i, k],
            device_id=(along(d, j + 1), node),
            device_id_type=MESH,
        )

    def ring_copy(i, d, s):
        return pltpu.make_async_remote_copy(
            src_ref=ring_out.at[i, lax.rem(s, 2), d],
            dst_ref=ring_in.at[i, s, d],
            send_sem=ring_send_sem.at[i, d, lax.rem(s, 2)],
            recv_sem=ring_recv_sem.at[i, d, s],
            device_id=(along(d, 1), node),
            device_id_type=MESH,
        )

    def wanted(shape, dim, d, core):
        at = lax.broadcasted_iota(jnp.int32, shape, dim)
        j = quotient(at, far_rows, shape[dim])
        place = at - j * far_rows
        pos = z + toward[d] * (relay + 1 + j)
        pos = jnp.where(pos < 0, pos + nz, pos)
        pos = jnp.where(pos >= nz, pos - nz, pos)
        place = place - core * cap
        held = (place >= 0) & (place < cap)
        return jnp.where(held, (pos * 2 + c) * cap + place, -5).astype(f32)

    def write_onehots(s):
        ids = lax.broadcasted_iota(jnp.int32, (rows, toks), 0).astype(f32)
        for d in ways:
            base = ((at_z(z + toward[d] * (relay - s)) * 2 + c) * rows).astype(f32)
            for h in (0, 1):
                onehots[rows * d : rows * (d + 1), toks * h : toks * (h + 1)] = (
                    (code[h, 0:1, :] == ids + base).astype(f32).astype(bf16)
                )

    def add_up(i):
        contrib[:, cols[i]] = jnp.dot(
            onehots[...], tok[:, cols[i]], preferred_element_type=f32
        )

    def own_terms(i):
        return contrib[:, cols[i]].reshape(2, rows, PIECE)

    def send_on(i, s, x):
        packed, levels = quantise(x)
        ref = ring_out.at[i, lax.rem(s, 2)]
        ref[:, 0:rows, :] = packed
        ref[:, rows : rows + 1, :] = levels
        for d in ways:
            ring_copy(i, d, s).start()

    def arrived(i, s):
        for d in ways:
            ring_copy(i, d, s).wait_recv()
        ref = ring_in.at[i, s]
        return unpack(ref[:, 0:rows, :], ref[:, rows : rows + 1, :])

    def relay_step(i):
        x = own_terms(i)
        if far_all:
            for k in range(far_all):
                far_copy(i, k).wait_recv()
            ref = far_in.at[i]
            ids = ref[:, both + 1 : both + 2, :]
            spread = unpack(ref[...], ref[:, both : both + 1, :])
            lane = lax.broadcasted_iota(jnp.int32, (1, LANES), 1)
            sub = lax.broadcasted_iota(jnp.int32, (rows, LANES), 0)
            placed = []
            for d in ways:
                ks = slice(far[LONGER] * d, far[LONGER] + far[SHORTER] * d)
                n = far[d] * far_rows
                ids_d = jnp.sum(ids[ks], axis=0) if n else jnp.zeros_like(lane)
                placing = ((jnp.where(lane < n, ids_d, -1)) == sub).astype(f32)
                parts = [spread[ks].reshape(n, PIECE)] if n else []
                if n < LANES:
                    parts.append(jnp.zeros((LANES - n, PIECE), f32))
                y = jnp.concatenate(parts, axis=0)
                top = y.astype(bf16)
                rest = (y - top.astype(f32)).astype(bf16)
                placing = placing.astype(bf16)
                placed.append(
                    jnp.dot(placing, top, preferred_element_type=f32)
                    + jnp.dot(placing, rest, preferred_element_type=f32)
                )
            x = x + jnp.stack(placed)
        send_on(i, 0, x)

    pair_code.wait_recv()
    write_onehots(0)
    at = 0
    for d in ways:
        n = far[d] * far_rows
        if not n:
            continue
        for h in (0, 1):
            slots_of = wanted((n, LANES), 0, d, h)
            far_onehot[at : at + n, toks * h : toks * (h + 1)] = jnp.concatenate(
                [
                    (slots_of == code[h, 1:2, LANES * k : LANES * (k + 1)]).astype(f32)
                    for k in range(toks // LANES)
                ],
                axis=1,
            ).astype(bf16)
        found = jnp.zeros((8, LANES), f32)
        for h in (0, 1):
            sub = lax.broadcasted_iota(jnp.int32, (toks, LANES), 0).astype(f32)
            choose = (wanted((1, LANES), 1, d, h) == sub).astype(f32)
            found = found + jnp.dot(
                jnp.broadcast_to(code[h, 2:3, :], (8, toks)).astype(bf16),
                choose.astype(bf16),
                preferred_element_type=f32,
            )
        lane = lax.broadcasted_iota(jnp.int32, (1, LANES), 1)
        which = quotient(lane, far_rows, LANES)
        ids = jnp.where(
            lane - which * far_rows < both, found[0:1, :].astype(jnp.int32), -1
        )
        for j in range(far[d]):
            far_ids[far[LONGER] * d + j] = jnp.where(which == j, ids, 0)
        at += n

    def tokens_in(i):
        if i == 0:
            own_tok.wait()

        @pl.loop(1, n_node)
        def _(j):
            tok_copy(i, j, True).wait_recv()

        tok[0:toks, cols[i]] = jnp.concatenate(
            [tok3[n, :, cols[i]].astype(f32) for n in range(n_node)], axis=0
        ).astype(bf16)
        pair_copy(i).start()

    def far_rows_out(i):
        pair_copy(i).wait_recv()
        if far_all:
            x = jnp.dot(far_onehot[...], tok[:, cols[i]], preferred_element_type=f32)
            packed, levels = quantise(x.reshape(far_all, far_rows, PIECE))
            at = lax.broadcasted_iota(jnp.int32, packed.shape, 1)
            far_out[i] = jnp.where(
                at == both,
                levels,
                jnp.where(at == both + 1, far_ids[...], packed),
            )
            for k in range(far_all):
                far_copy(i, k).start()
        add_up(i)

    for i in range(pieces):
        tokens_in(i)
        if i:
            far_rows_out(i - 1)
    far_rows_out(pieces - 1)
    for i in range(pieces):
        relay_step(i)
    write_onehots(1)
    for i in range(pieces):
        add_up(i)

    @pl.loop(1, relay)
    def _(s):
        for i in range(pieces):
            for d in ways:
                ring_copy(i, d, s - 1).wait_recv()
                ref = ring_in.at[i, s - 1, d]
                x = unpack(ref[0:rows, :], ref[rows : rows + 1, :])
                x = x + contrib[rows * d : rows * (d + 1), cols[i]]

                @pl.when(s >= 2)
                def _(i=i, d=d):
                    ring_copy(i, d, s - 2).wait_send()

                packed, levels = quantise(x)
                ref = ring_out.at[i, lax.rem(s, 2), d]
                ref[0:rows, :] = packed
                ref[rows : rows + 1, :] = levels
                ring_copy(i, d, s).start()
        write_onehots(s + 1)
        for i in range(pieces):
            add_up(i)

    for i in range(pieces):
        x = arrived(i, relay - 1)
        out[:, cols[i]] = x[0] + x[1] + contrib[0:rows, cols[i]]

    @pl.loop(1, n_node)
    def _(j):
        slot_copy(j, False).wait_send()
        for i in range(pieces):
            tok_copy(i, j, False).wait_send()

    pair_code.wait_send()
    for i in range(pieces):
        pair_copy(i).wait_send()
        for k in range(far_all):
            far_copy(i, k).wait_send()
        for d in ways:
            for s in range(max(relay - 2, 0), relay):
                ring_copy(i, d, s).wait_send()


def summed(grads, merge_slot, slot_row, n_group, n_node, rows):
    toks, width = grads.shape
    blk = toks // n_node
    pieces = width // PIECE
    assert width == PIECE * pieces
    _, relay, far, both, far_rows = plan(n_group, toks)
    far_all = max(far[LONGER] + far[SHORTER], 1)
    assert far[LONGER] * far_rows <= LANES
    cfg = (n_group, n_node, rows, toks, width)
    i32, f32, bf16 = jnp.int32, jnp.float32, jnp.bfloat16
    vmem, dma = pltpu.VMEM, pltpu.SemaphoreType.DMA
    return pl.pallas_call(
        functools.partial(kernel, cfg),
        out_shape=jax.ShapeDtypeStruct((rows, width), f32),
        in_specs=[
            pl.BlockSpec(memory_space=pltpu.HBM),
            pl.BlockSpec(memory_space=vmem),
            pl.BlockSpec(memory_space=vmem),
        ],
        out_specs=pl.BlockSpec(memory_space=vmem),
        scratch_shapes=[
            vmem((n_node, blk, width), bf16),
            vmem((n_node, toks // LANES, LANES), i32),
            vmem((2 * toks, width), bf16),
            vmem((2, 3, toks), f32),
            vmem((n_node, toks), i32),
            vmem((2 * rows, 2 * toks), bf16),
            vmem((2 * rows, width), f32),
            vmem((far_all * far_rows, 2 * toks), bf16),
            vmem((far_all, 1, LANES), i32),
            vmem((pieces, far_all, far_rows, LANES), i32),
            vmem((pieces, far_all, far_rows, LANES), i32),
            vmem((pieces, 2, 2, rows + 1, LANES), i32),
            vmem((pieces, relay, 2, rows + 1, LANES), i32),
            dma((n_node,)),
            dma((n_node,)),
            dma((pieces, n_node)),
            dma((pieces, n_node)),
            dma((2,)),
            dma((pieces + 1,)),
            dma((pieces + 1,)),
            dma((pieces, far_all)),
            dma((pieces, far_all)),
            dma((pieces, 2, 2)),
            dma((pieces, 2, relay)),
        ],
        compiler_params=pltpu.CompilerParams(
            collective_id=0, has_side_effects=True, vmem_limit_bytes=40 * 1024 * 1024
        ),
        name="ring_sums",
    )(
        grads.reshape(n_node, blk, width),
        merge_slot.reshape(toks // LANES, LANES),
        slot_row.reshape(toks // LANES, LANES),
    )


def on_device(n_group, n_node, grads, merge_slot, slot_row, params, moment, second):
    grad = summed(grads, merge_slot, slot_row, n_group, n_node, params.shape[0])
    new_moment = 0.9 * moment + 0.1 * grad
    new_second = 0.999 * second + 0.001 * grad * grad
    first_fix = 1.0 - 0.9**10
    second_fix = 1.0 - 0.999**10
    new_params = params - 0.1 * (new_moment / first_fix) / (
        jnp.sqrt(new_second / second_fix) + 1e-08
    )
    return (new_params, new_moment, new_second)


def solution(mesh):
    whole, flat = P(("group", "node"), None), P(("group", "node"))
    return jax.shard_map(
        functools.partial(on_device, mesh.shape["group"], mesh.shape["node"]),
        mesh=mesh,
        in_specs=(whole, flat, flat, whole, whole, whole),
        out_specs=(whole, whole, whole),
        check_vma=False,
    )
```

```python
import functools

import jax
import jax.numpy as jnp
from jax import lax
from jax.experimental import pallas as pl
from jax.experimental.pallas import tpu as pltpu
from jax.sharding import PartitionSpec as P

MESH = pl.DeviceIdType.MESH
LANES = 128
PIECE = 2 * LANES
FINE = 64.0
TOP = 32600.0
LONGER, SHORTER = 0, 1


def quotient(x, by, limit):
    magic = -(-65536 // by)
    assert all((v * magic) >> 16 == v // by for v in range(limit))
    return (x * magic) >> 16


def low_half(p):
    return (p << 16) >> 16


def pack(hi, lo):
    return (hi << 16) | (lo & 0xFFFF)


def nearest(x):
    return jnp.floor(x + 0.5).astype(jnp.int32)


def halves(x):
    return x[..., :LANES], x[..., LANES:]


def quantise(x):
    most = jnp.max(jnp.abs(x), axis=-2, keepdims=True)
    level = jnp.ceil(jnp.log2(jnp.maximum(most, 1e-30)) * FINE)
    q = nearest(x * (jnp.exp2(level * (-1.0 / FINE)) * TOP))
    return pack(*halves(q)), pack(*halves(level.astype(jnp.int32)))


def step_size(level):
    return jnp.exp2(level.astype(jnp.float32) * (1.0 / FINE)) * (1.0 / TOP)


def unpack(packed, levels):
    hi = (packed >> 16).astype(jnp.float32) * step_size(levels >> 16)
    lo = low_half(packed).astype(jnp.float32) * step_size(low_half(levels))
    return jnp.concatenate([hi, lo], axis=-1)


def plan(n_group, toks):
    nz = n_group // 2
    hops = (nz // 2, nz // 2 - 1)
    relay = 11 if nz == 32 else max(nz // 2 - 2, 1)
    far = (hops[0] - relay, hops[1] - relay)
    both = 2 * (toks // n_group)
    return nz, relay, far, both, -(-(both + 2) // 8) * 8


def kernel(
    cfg,
    grads,
    slots,
    slot_row,
    out,
    tok3,
    slot_in,
    tok,
    code,
    slot_mat,
    onehots,
    contrib,
    far_onehot,
    far_ids,
    far_out,
    far_in,
    ring_out,
    ring_in,
    slot_send_sem,
    slot_recv_sem,
    tok_send_sem,
    tok_recv_sem,
    local_sem,
    pair_send_sem,
    pair_recv_sem,
    far_send_sem,
    far_recv_sem,
    ring_send_sem,
    ring_recv_sem,
):
    n_group, n_node, rows, toks, width = cfg
    nz, relay, far, both, far_rows = plan(n_group, toks)
    f32, bf16 = jnp.float32, jnp.bfloat16
    pieces = width // PIECE
    blk = toks // n_node
    cap = toks // n_group
    cols = [slice(PIECE * i, PIECE * (i + 1)) for i in range(pieces)]
    ways = (LONGER, SHORTER)
    far_all = far[LONGER] + far[SHORTER]

    group = lax.axis_index("group")
    node = lax.axis_index("node")
    z, c = lax.div(group, 2), lax.rem(group, 2)
    sign = 1 - 2 * c
    toward = (sign, -sign)

    def at_z(pos):
        return lax.rem(pos + 2 * nz, nz)

    def along(d, distance):
        return at_z(z + toward[d] * distance) * 2 + c

    partner = (z * 2 + 1 - c, node)

    far_in[...] = jnp.zeros_like(far_in)
    barrier = pltpu.get_barrier_semaphore()

    @pl.loop(1, n_node)
    def _(j):
        pl.semaphore_signal(
            barrier,
            inc=1,
            device_id=(group, lax.rem(node + j, n_node)),
            device_id_type=MESH,
        )

    near = max(far[LONGER], 1)
    pl.semaphore_signal(barrier, inc=1, device_id=partner, device_id_type=MESH)
    for d in ways:

        @pl.loop(1, near + 1)
        def _(j, d=d):
            pl.semaphore_signal(
                barrier, inc=1, device_id=(along(d, j), node), device_id_type=MESH
            )

    pl.semaphore_wait(barrier, n_node + 2 * near)

    def slot_copy(j, landing):
        peer = lax.rem(node + j, n_node)
        at = peer if landing else node
        return pltpu.make_async_remote_copy(
            src_ref=slots,
            dst_ref=slot_in.at[at],
            send_sem=slot_send_sem.at[j],
            recv_sem=slot_recv_sem.at[at],
            device_id=(group, peer),
            device_id_type=MESH,
        )

    def tok_copy(i, j, landing):
        peer = lax.rem(node + j, n_node)
        at = peer if landing else node
        return pltpu.make_async_remote_copy(
            src_ref=grads.at[peer, :, cols[i]],
            dst_ref=tok3.at[at, :, cols[i]],
            send_sem=tok_send_sem.at[i, j],
            recv_sem=tok_recv_sem.at[i, at],
            device_id=(group, peer),
            device_id_type=MESH,
        )

    own_tok = pltpu.make_async_copy(grads.at[node], tok3.at[node], local_sem.at[0])
    own_slot = pltpu.make_async_copy(slots, slot_in.at[node], local_sem.at[1])

    @pl.loop(1, n_node)
    def _(j):
        slot_copy(j, False).start()

    own_slot.start()
    own_tok.start()
    for i in range(pieces):

        @pl.loop(1, n_node)
        def _(j, i=i):
            tok_copy(i, j, False).start()

    own_slot.wait()

    @pl.loop(1, n_node)
    def _(j):
        slot_copy(j, True).wait_recv()

    for n in range(n_node):
        for k in range(toks // LANES):
            slot_mat[n : n + 1, k * LANES : (k + 1) * LANES] = slot_in[n, k : k + 1, :]
    slot = slot_mat[...]
    owner = quotient(slot, cap, toks)
    place = slot - owner * cap
    lane = lax.broadcasted_iota(jnp.int32, (toks, toks), 1)
    sub = lax.broadcasted_iota(jnp.int32, (toks, toks), 0)
    mine = sub - node * blk == lane - quotient(lane, blk, toks) * blk
    mine = mine.astype(f32).astype(bf16)
    lane = lax.broadcasted_iota(jnp.int32, (n_node, toks), 1)
    source = lax.broadcasted_iota(jnp.int32, (n_node, toks), 0)
    here = (quotient(lane, blk, toks) == source).astype(f32)

    def pick(values):
        moved = jnp.dot(
            values.astype(f32).astype(bf16), mine, preferred_element_type=f32
        )
        return jnp.sum(moved * here, axis=0, keepdims=True)

    owner = pick(owner)
    index = owner * float(cap) + pick(place)
    onehot = (index == sub.astype(f32)).astype(f32).astype(bf16)
    table = jnp.concatenate(
        [slot_row[k : k + 1, :] for k in range(toks // LANES)], axis=1
    ).astype(f32)
    row = jnp.dot(
        jnp.broadcast_to(table, (8, toks)).astype(bf16),
        onehot,
        preferred_element_type=f32,
    )
    code[0, 0:1, :] = owner * float(rows) + row[0:1, :]
    code[0, 1:2, :] = index
    code[0, 2:3, :] = table

    pair_code = pltpu.make_async_remote_copy(
        src_ref=code.at[0],
        dst_ref=code.at[1],
        send_sem=pair_send_sem.at[pieces],
        recv_sem=pair_recv_sem.at[pieces],
        device_id=partner,
        device_id_type=MESH,
    )
    pair_code.start()

    def pair_copy(i):
        return pltpu.make_async_remote_copy(
            src_ref=tok.at[0:toks, cols[i]],
            dst_ref=tok.at[toks : 2 * toks, cols[i]],
            send_sem=pair_send_sem.at[i],
            recv_sem=pair_recv_sem.at[i],
            device_id=partner,
            device_id_type=MESH,
        )

    def far_copy(i, k):
        d, j = (LONGER, k) if k < far[LONGER] else (SHORTER, k - far[LONGER])
        return pltpu.make_async_remote_copy(
            src_ref=far_out.at[i, k, 0 : both + 2],
            dst_ref=far_in.at[i, k, 0 : both + 2],
            send_sem=far_send_sem.at[i, k],
            recv_sem=far_recv_sem.at[i, k],
            device_id=(along(d, j + 1), node),
            device_id_type=MESH,
        )

    def ring_copy(i, d, s):
        return pltpu.make_async_remote_copy(
            src_ref=ring_out.at[i, lax.rem(s, 2), d],
            dst_ref=ring_in.at[i, s, d],
            send_sem=ring_send_sem.at[i, d, lax.rem(s, 2)],
            recv_sem=ring_recv_sem.at[i, d, s],
            device_id=(along(d, 1), node),
            device_id_type=MESH,
        )

    def wanted(shape, dim, d, core):
        at = lax.broadcasted_iota(jnp.int32, shape, dim)
        j = quotient(at, far_rows, shape[dim])
        place = at - j * far_rows
        pos = z + toward[d] * (relay + 1 + j)
        pos = jnp.where(pos < 0, pos + nz, pos)
        pos = jnp.where(pos >= nz, pos - nz, pos)
        place = place - core * cap
        held = (place >= 0) & (place < cap)
        return jnp.where(held, (pos * 2 + c) * cap + place, -5).astype(f32)

    def write_onehots(s):
        ids = lax.broadcasted_iota(jnp.int32, (rows, toks), 0).astype(f32)
        for d in ways:
            base = ((at_z(z + toward[d] * (relay - s)) * 2 + c) * rows).astype(f32)
            for h in (0, 1):
                onehots[rows * d : rows * (d + 1), toks * h : toks * (h + 1)] = (
                    (code[h, 0:1, :] == ids + base).astype(f32).astype(bf16)
                )

    def add_up(i):
        contrib[:, cols[i]] = jnp.dot(
            onehots[...], tok[:, cols[i]], preferred_element_type=f32
        )

    def own_terms(i):
        return contrib[:, cols[i]].reshape(2, rows, PIECE)

    def send_on(i, s, x):
        packed, levels = quantise(x)
        ref = ring_out.at[i, lax.rem(s, 2)]
        ref[:, 0:rows, :] = packed
        ref[:, rows : rows + 1, :] = levels
        for d in ways:
            ring_copy(i, d, s).start()

    def arrived(i, s):
        for d in ways:
            ring_copy(i, d, s).wait_recv()
        ref = ring_in.at[i, s]
        return unpack(ref[:, 0:rows, :], ref[:, rows : rows + 1, :])

    def relay_step(i):
        x = own_terms(i)
        if far_all:
            for k in range(far_all):
                far_copy(i, k).wait_recv()
            ref = far_in.at[i]
            ids = ref[:, both + 1 : both + 2, :]
            spread = unpack(ref[...], ref[:, both : both + 1, :])
            lane = lax.broadcasted_iota(jnp.int32, (1, LANES), 1)
            sub = lax.broadcasted_iota(jnp.int32, (rows, LANES), 0)
            placed = []
            for d in ways:
                ks = slice(far[LONGER] * d, far[LONGER] + far[SHORTER] * d)
                n = far[d] * far_rows
                ids_d = jnp.sum(ids[ks], axis=0) if n else jnp.zeros_like(lane)
                placing = ((jnp.where(lane < n, ids_d, -1)) == sub).astype(f32)
                parts = [spread[ks].reshape(n, PIECE)] if n else []
                if n < LANES:
                    parts.append(jnp.zeros((LANES - n, PIECE), f32))
                y = jnp.concatenate(parts, axis=0)
                top = y.astype(bf16)
                rest = (y - top.astype(f32)).astype(bf16)
                placing = placing.astype(bf16)
                placed.append(
                    jnp.dot(placing, top, preferred_element_type=f32)
                    + jnp.dot(placing, rest, preferred_element_type=f32)
                )
            x = x + jnp.stack(placed)
        send_on(i, 0, x)

    pair_code.wait_recv()
    write_onehots(0)
    at = 0
    for d in ways:
        n = far[d] * far_rows
        if not n:
            continue
        for h in (0, 1):
            slots_of = wanted((n, LANES), 0, d, h)
            far_onehot[at : at + n, toks * h : toks * (h + 1)] = jnp.concatenate(
                [
                    (slots_of == code[h, 1:2, LANES * k : LANES * (k + 1)]).astype(f32)
                    for k in range(toks // LANES)
                ],
                axis=1,
            ).astype(bf16)
        found = jnp.zeros((8, LANES), f32)
        for h in (0, 1):
            sub = lax.broadcasted_iota(jnp.int32, (toks, LANES), 0).astype(f32)
            choose = (wanted((1, LANES), 1, d, h) == sub).astype(f32)
            found = found + jnp.dot(
                jnp.broadcast_to(code[h, 2:3, :], (8, toks)).astype(bf16),
                choose.astype(bf16),
                preferred_element_type=f32,
            )
        lane = lax.broadcasted_iota(jnp.int32, (1, LANES), 1)
        which = quotient(lane, far_rows, LANES)
        ids = jnp.where(
            lane - which * far_rows < both, found[0:1, :].astype(jnp.int32), -1
        )
        for j in range(far[d]):
            far_ids[far[LONGER] * d + j] = jnp.where(which == j, ids, 0)
        at += n

    def tokens_in(i):
        if i == 0:
            own_tok.wait()

        @pl.loop(1, n_node)
        def _(j):
            tok_copy(i, j, True).wait_recv()

        tok[0:toks, cols[i]] = jnp.concatenate(
            [tok3[n, :, cols[i]].astype(f32) for n in range(n_node)], axis=0
        ).astype(bf16)
        pair_copy(i).start()

    def far_rows_out(i):
        pair_copy(i).wait_recv()
        if far_all:
            x = jnp.dot(far_onehot[...], tok[:, cols[i]], preferred_element_type=f32)
            packed, levels = quantise(x.reshape(far_all, far_rows, PIECE))
            at = lax.broadcasted_iota(jnp.int32, packed.shape, 1)
            far_out[i] = jnp.where(
                at == both,
                levels,
                jnp.where(at == both + 1, far_ids[...], packed),
            )
            for k in reversed(range(far_all)):
                far_copy(i, k).start()
        add_up(i)

    for i in range(pieces):
        tokens_in(i)
        if i:
            far_rows_out(i - 1)
    far_rows_out(pieces - 1)
    for i in range(pieces):
        relay_step(i)
    write_onehots(1)
    for i in range(pieces):
        add_up(i)

    @pl.loop(1, relay)
    def _(s):
        for i in range(pieces):
            for d in ways:
                ring_copy(i, d, s - 1).wait_recv()
                ref = ring_in.at[i, s - 1, d]
                x = unpack(ref[0:rows, :], ref[rows : rows + 1, :])
                x = x + contrib[rows * d : rows * (d + 1), cols[i]]

                @pl.when(s >= 2)
                def _(i=i, d=d):
                    ring_copy(i, d, s - 2).wait_send()

                packed, levels = quantise(x)
                ref = ring_out.at[i, lax.rem(s, 2), d]
                ref[0:rows, :] = packed
                ref[rows : rows + 1, :] = levels
                ring_copy(i, d, s).start()
        write_onehots(s + 1)
        for i in range(pieces):
            add_up(i)

    for i in range(pieces):
        x = arrived(i, relay - 1)
        out[:, cols[i]] = x[0] + x[1] + contrib[0:rows, cols[i]]

    @pl.loop(1, n_node)
    def _(j):
        slot_copy(j, False).wait_send()
        for i in range(pieces):
            tok_copy(i, j, False).wait_send()

    pair_code.wait_send()
    for i in range(pieces):
        pair_copy(i).wait_send()
        for k in range(far_all):
            far_copy(i, k).wait_send()
        for d in ways:
            for s in range(max(relay - 2, 0), relay):
                ring_copy(i, d, s).wait_send()


def summed(grads, merge_slot, slot_row, n_group, n_node, rows):
    toks, width = grads.shape
    blk = toks // n_node
    pieces = width // PIECE
    assert width == PIECE * pieces
    _, relay, far, both, far_rows = plan(n_group, toks)
    far_all = max(far[LONGER] + far[SHORTER], 1)
    assert far[LONGER] * far_rows <= LANES
    cfg = (n_group, n_node, rows, toks, width)
    i32, f32, bf16 = jnp.int32, jnp.float32, jnp.bfloat16
    vmem, dma = pltpu.VMEM, pltpu.SemaphoreType.DMA
    return pl.pallas_call(
        functools.partial(kernel, cfg),
        out_shape=jax.ShapeDtypeStruct((rows, width), f32),
        in_specs=[
            pl.BlockSpec(memory_space=pltpu.HBM),
            pl.BlockSpec(memory_space=vmem),
            pl.BlockSpec(memory_space=vmem),
        ],
        out_specs=pl.BlockSpec(memory_space=vmem),
        scratch_shapes=[
            vmem((n_node, blk, width), bf16),
            vmem((n_node, toks // LANES, LANES), i32),
            vmem((2 * toks, width), bf16),
            vmem((2, 3, toks), f32),
            vmem((n_node, toks), i32),
            vmem((2 * rows, 2 * toks), bf16),
            vmem((2 * rows, width), f32),
            vmem((far_all * far_rows, 2 * toks), bf16),
            vmem((far_all, 1, LANES), i32),
            vmem((pieces, far_all, far_rows, LANES), i32),
            vmem((pieces, far_all, far_rows, LANES), i32),
            vmem((pieces, 2, 2, rows + 1, LANES), i32),
            vmem((pieces, relay, 2, rows + 1, LANES), i32),
            dma((n_node,)),
            dma((n_node,)),
            dma((pieces, n_node)),
            dma((pieces, n_node)),
            dma((2,)),
            dma((pieces + 1,)),
            dma((pieces + 1,)),
            dma((pieces, far_all)),
            dma((pieces, far_all)),
            dma((pieces, 2, 2)),
            dma((pieces, 2, relay)),
        ],
        compiler_params=pltpu.CompilerParams(
            collective_id=0, has_side_effects=True, vmem_limit_bytes=40 * 1024 * 1024
        ),
        name="ring_sums",
    )(
        grads.reshape(n_node, blk, width),
        merge_slot.reshape(toks // LANES, LANES),
        slot_row.reshape(toks // LANES, LANES),
    )


def on_device(n_group, n_node, grads, merge_slot, slot_row, params, moment, second):
    grad = summed(grads, merge_slot, slot_row, n_group, n_node, params.shape[0])
    new_moment = 0.9 * moment + 0.1 * grad
    new_second = 0.999 * second + 0.001 * grad * grad
    first_fix = 1.0 - 0.9**10
    second_fix = 1.0 - 0.999**10
    new_params = params - 0.1 * (new_moment / first_fix) / (
        jnp.sqrt(new_second / second_fix) + 1e-08
    )
    return (new_params, new_moment, new_second)


def solution(mesh):
    whole, flat = P(("group", "node"), None), P(("group", "node"))
    return jax.shard_map(
        functools.partial(on_device, mesh.shape["group"], mesh.shape["node"]),
        mesh=mesh,
        in_specs=(whole, flat, flat, whole, whole, whole),
        out_specs=(whole, whole, whole),
        check_vma=False,
    )
```
